256 devices in a mesh: row: 32 (over x, z_hi, core), col: 8 (over y, z_lo).
Axes of the slice: x: 4, y: 4, z: 8 (z_hi: 4, z_lo: 2; z = z_hi * 2 + z_lo), core: 2. Of those that a mesh axis runs over, the one named last changes fastest.
Arguments:
- activations: bfloat16 [1024, 18432], P('row', 'col'), may hold values from -6 to 6
- out_grads: bfloat16 [1024, 7168], P('col', 'row'), may hold values from -1 to 1
- query_acts: bfloat16 [64, 18432], P('row', 'col'), may hold values from -6 to 6
- query_grads: bfloat16 [64, 7168], P('col', 'row'), may hold values from -1 to 1
- basis_in: bfloat16 [18432, 18432], P('col', 'row'), may hold values from -0.046875 to 0.046875
- basis_out: bfloat16 [7168, 7168], P('row', 'col'), may hold values from -0.0625 to 0.0625
- damping: float32 [1], replicated, may hold values from 0.1 to 1
Outputs:
- corrected: float32 [7168, 18432], P('col', 'row')
The draws below stay inside these ranges and needn't reach their ends.
All inputs are finite; a program needn't handle non-finite values.
Results may differ from the reference program's by a relative error of at most 0.0044.
Values may be sent and summed in bfloat16 or wider, within the bound.
No kernel may reach another device: no remote copies, remote signals or barrier semaphores. Data moves between devices by JAX's collectives and lax.ppermute only.
A program may use at most 64 MiB of HBM per device.

```python
import math
import jax
import jax.numpy as jnp
from jax import lax

DIN = 18432
DOUT = 7168
TL = 64
QTOK = 64
EXAMPLES = 16
TOK = 1024


def block_scale(key, extent, cuts, smallest, high):
    factor_of = 1.0
    for position, parts in cuts:
        steps = jax.random.uniform(jax.random.fold_in(jax.random.fold_in(key, 6), position), (parts,), jnp.float32, smallest / len(cuts), high / len(cuts))
        factor_of = factor_of * jnp.repeat(jnp.exp(steps), extent[position] // parts).reshape((-1,) + (1,) * (len(extent) - 1 - position))
    return factor_of


def noise(stream_key, extent, width, limit, split=(), dtype=jnp.bfloat16):
    values = width * jax.random.normal(stream_key, extent, jnp.float32)
    if split:
        values = values * block_scale(stream_key, extent, split, -0.22, 0.18)
    return jnp.clip(values, -limit, limit).astype(dtype)


def setup_inputs(seed: int = 0) -> dict:
    splits = jax.random.split(jax.random.key(seed), 8)
    activations = noise(splits[0], (TOK, DIN), 1.0, 6.0, ((0, 32), (1, 8)))
    out_grads = noise(splits[1], (TOK, DOUT), 0.125, 1.0, ((0, 8), (1, 32)))
    query_acts = noise(splits[2], (QTOK, DIN), 1.0, 6.0, ((0, 32), (1, 8)))
    query_grads = noise(splits[3], (QTOK, DOUT), 0.125, 1.0, ((0, 8), (1, 32)))
    basis_in = noise(splits[4], (DIN, DIN), DIN ** -0.5, 0.046875, ((0, 8), (1, 32)))
    basis_out = noise(splits[5], (DOUT, DOUT), DOUT ** -0.5, 0.0625, ((0, 32), (1, 8)))
    damping = jnp.clip(jnp.exp(jax.random.uniform(splits[6], (1,), jnp.float32, math.log(0.1), math.log(1.0))), 0.1, 1.0)
    return {"activations": activations, "out_grads": out_grads, "query_acts": query_acts, "query_grads": query_grads, "basis_in": basis_in, "basis_out": basis_out, "damping": damping}


def reference(activations, out_grads, query_acts, query_grads, basis_in, basis_out, damping):
    rot_act = jnp.dot(activations, basis_in, preferred_element_type=jnp.float32).astype(jnp.bfloat16)
    rot_grad = jnp.dot(out_grads, basis_out, preferred_element_type=jnp.float32).astype(jnp.bfloat16)
    q_act = jnp.dot(query_acts, basis_in, preferred_element_type=jnp.float32).astype(jnp.bfloat16)
    q_grad = jnp.dot(query_grads, basis_out, preferred_element_type=jnp.float32).astype(jnp.bfloat16)

    def accumulate(index, total):
        act_block = lax.dynamic_slice_in_dim(rot_act, index * TL, TL, 0)
        grad_block = lax.dynamic_slice_in_dim(rot_grad, index * TL, TL, 0)
        outer = lax.dot_general(grad_block, act_block, (((0,), (0,)), ((), ())), preferred_element_type=jnp.float32)
        return total + outer * outer

    moment = lax.fori_loop(0, EXAMPLES, accumulate, jnp.zeros((DOUT, DIN), jnp.float32)) / EXAMPLES
    query = lax.dot_general(q_grad, q_act, (((0,), (0,)), ((), ())), preferred_element_type=jnp.float32)
    return query / (moment + damping[0])
```

```python
import functools
import jax
import jax.numpy as jnp
from jax import lax
from jax.experimental import pallas as pl
from jax.experimental.pallas import tpu as pltpu
from jax.sharding import Mesh
from jax.sharding import PartitionSpec as P

EXAMPLES = 16
ROW = ("x", "zh", "core")
COL = ("y", "zl")
BF16 = jnp.bfloat16
WIRE = jnp.float16
F32 = jnp.float32
ROWS = 32
PIECE = 40
TOKENS_FIRST = (((0,), (0,)), ((), ()))


def shifted(value, axis, by):
    size = lax.axis_size(axis)
    return lax.ppermute(value, axis, [(i, (i + by) % size) for i in range(size)])


def swapped(value):
    return shifted(value, "core", 1)


def ring_gather(value, axis):
    back = shifted(value, axis, 1)
    ahead = shifted(value, axis, -1)
    half = value.shape[-1] // 256 * 128
    left = shifted(back[..., :half], axis, 1)
    right = shifted(ahead[..., half:], axis, -1)
    return value, back, ahead, jnp.concatenate([left, right], -1)


def copy_for_each(value, axis):
    peers = lax.axis_size(axis)
    return lax.all_to_all(
        jnp.broadcast_to(value[None], (peers, *value.shape)), axis, 0, 0, tiled=True
    )


def padded(value, rows):
    return jnp.pad(value, ((0, rows - value.shape[0]), (0, 0)))


def summed_share(partial, axis, scale):
    arrived = lax.all_to_all((partial * scale).astype(WIRE), axis, 0, 0, tiled=True)
    return (arrived.astype(F32).sum(0) * (1 / scale)).astype(BF16)


def final_kernel(place, damping, act_own, act_other, grad_own, grad_other, out):
    core, x, zh = place[0], place[1], place[2]
    first = core == 0
    height, width = out.shape
    tile = 256

    for left in range(0, width, tile):
        cols = slice(left, min(left + tile, width))

        def in_turn(own, other):
            return [jnp.where(first, own, other), jnp.where(first, other, own)]

        total = None
        query_act, query_grad = [], []
        for block in range(EXAMPLES // 2):
            for source, part in ((grad_own, core), (grad_other, 1 - core)):
                example = 2 * block + part
                slot_x = (example // 4 - x + 4) % 4
                slot_z = (example % 4 - zh + 4) % 4
                slot_x = jnp.where(slot_x == 0, 0, slot_x % 3 + 1)
                slot_z = jnp.where(slot_z == 0, 0, slot_z % 3 + 1)
                slot = slot_x * 4 + slot_z
                act = jnp.concatenate(
                    in_turn(act_own[slot, :ROWS, cols], act_other[slot, :ROWS, cols]), 0
                )
                grad = jnp.concatenate(
                    [source[2 * block, :ROWS, :], source[2 * block + 1, :ROWS, :]], 0
                )
                outer = lax.dot_general(grad, act, TOKENS_FIRST, preferred_element_type=F32)
                total = outer * outer if total is None else total + outer * outer
                query_act += in_turn(act_own[slot, ROWS:, cols], act_other[slot, ROWS:, cols])
                query_grad += [source[2 * block, ROWS:, :], source[2 * block + 1, ROWS:, :]]
        query = lax.dot_general(
            jnp.concatenate(query_grad, 0),
            jnp.concatenate(query_act, 0),
            TOKENS_FIRST,
            preferred_element_type=F32,
        )
        out[:, cols] = query / (total * (1 / EXAMPLES) + damping[0])


def corrected(place, damping, act_own, act_other, grad_own, grad_other):
    width, height = act_own.shape[2], grad_own.shape[2]
    return pl.pallas_call(
        final_kernel,
        out_shape=jax.ShapeDtypeStruct((height, width), F32),
        in_specs=[pl.BlockSpec(memory_space=pltpu.SMEM)] * 2
        + [pl.BlockSpec(memory_space=pltpu.VMEM)] * 4,
        out_specs=pl.BlockSpec(memory_space=pltpu.VMEM),
        compiler_params=pltpu.CompilerParams(vmem_limit_bytes=40 * 2**20),
        name="corrected",
    )(place, damping, act_own, act_other, grad_own, grad_other)


def shards(activations, out_grads, query_acts, query_grads, basis_in, basis_out, damping):
    core = lax.axis_index("core")
    width_in = basis_in.shape[1]
    width_out = basis_out.shape[1]

    basis_in_both = jnp.concatenate([basis_in, swapped(basis_in)], 1)
    basis_out_both = jnp.concatenate([basis_out, swapped(basis_out)], 0)

    acts = jnp.concatenate([activations, query_acts, jnp.zeros((6, activations.shape[1]), BF16)], 0)
    along_z = jnp.stack(ring_gather(acts, "zh"))
    along_x = jnp.concatenate(ring_gather(along_z, "x"), 0)
    gathered_in = along_x.reshape(-1, acts.shape[1])

    def half(which):
        rows = out_grads.shape[0] // 2
        q_rows = query_grads.shape[0] // 2
        train = lax.dynamic_slice_in_dim(out_grads, which * rows, rows, 0)
        query = lax.dynamic_slice_in_dim(query_grads, which * q_rows, q_rows, 0)
        pieces = []
        for i in range(2):
            pieces.append(train[i * ROWS : (i + 1) * ROWS])
            pieces.append(padded(query[i * 2 : (i + 1) * 2], PIECE - ROWS))
        return jnp.concatenate(pieces, 0)

    grads = jnp.concatenate([half(core), swapped(half(1 - core))], 1)
    gathered_out = copy_for_each(grads, COL).reshape(-1, grads.shape[1])

    partial_out = jnp.dot(gathered_out, basis_out_both, preferred_element_type=F32)
    share_out = summed_share(partial_out.reshape(16, PIECE, width_out), ("x", "zh"), 2.0**11)
    grad_own = copy_for_each(share_out, "zh")
    grad_own = copy_for_each(grad_own, "x").reshape(16, PIECE, width_out)
    grad_other = swapped(grad_own)

    partial_in = jnp.dot(gathered_in, basis_in_both, preferred_element_type=F32)
    share_in = summed_share(partial_in.reshape(8, 2 * PIECE, 2 * width_in), COL, 2.0**6)
    act_both = copy_for_each(share_in, COL).reshape(16, PIECE, 2 * width_in)
    act_own = act_both[:, :, :width_in]
    act_other = swapped(act_both[:, :, width_in:])

    place = jnp.stack([core, lax.axis_index("x"), lax.axis_index("zh")]).astype(jnp.int32)
    return corrected(place, damping, act_own, act_other, grad_own, grad_other)


def solution(mesh):
    finer = Mesh(mesh.devices.reshape(4, 4, 2, 4, 2), (*ROW, *COL))
    placed = (
        P(ROW, COL),
        P(COL, ROW),
        P(ROW, COL),
        P(COL, ROW),
        P(COL, ROW),
        P(ROW, COL),
        P(),
    )
    return jax.shard_map(
        shards, mesh=finer, in_specs=placed, out_specs=P(COL, ROW), check_vma=False
    )
```

```python
import functools
import jax
import jax.numpy as jnp
from jax import lax
from jax.experimental import pallas as pl
from jax.experimental.pallas import tpu as pltpu
from jax.sharding import Mesh
from jax.sharding import PartitionSpec as P

EXAMPLES = 16
ROW = ("x", "zh", "core")
COL = ("y", "zl")
BF16 = jnp.bfloat16
WIRE = jnp.float16
F32 = jnp.float32
SCALE_IN = 2.0**6
SCALE_OUT = 2.0**11
SCALE_OUT_X = 2.0**9
TOKENS_FIRST = (((0,), (0,)), ((), ()))
LAST_LAST = (((1,), (1,)), ((), ()))
VMEM = pl.BlockSpec(memory_space=pltpu.VMEM)
SMEM = pl.BlockSpec(memory_space=pltpu.SMEM)
ANY = pl.BlockSpec(memory_space=pl.ANY)
HBM = pl.BlockSpec(memory_space=pltpu.HBM)


NO_COST = pl.CostEstimate(flops=0, bytes_accessed=0, transcendentals=0)


def params(mib):
    return pltpu.CompilerParams(vmem_limit_bytes=mib * 2**20)


def from_ahead(value, axis, by):
    size = lax.axis_size(axis)
    return lax.ppermute(value, axis, [((i + by) % size, i) for i in range(size)])


def swapped(value):
    return from_ahead(value, "core", 1)


def exchanged(blocks, axis):
    return lax.all_to_all(blocks, axis, 0, 0, tiled=True)


def shares_kernel(place, own, other, earlier, out):
    first = place[0] == 0
    lower = jnp.where(first, own[...], other[...])
    upper = jnp.where(first, other[...], own[...])
    for peer in range(out.shape[0]):
        out[peer, 0] = lower
        out[peer, 1] = upper


def shares_for_each(place, own, other, peers, earlier):
    return pl.pallas_call(
        shares_kernel,
        out_shape=jax.ShapeDtypeStruct((peers, 2, *own.shape), own.dtype),
        in_specs=[SMEM, VMEM, VMEM, ANY],
        out_specs=VMEM,
        cost_estimate=NO_COST,
        compiler_params=params(4),
        name="shares",
    )(place, own, other, earlier)


def both_kernel(own, other, earlier, out):
    for peer in range(out.shape[0]):
        out[peer, 0] = own[...]
        out[peer, 1] = other[...]


def both_for_each(own, other, peers, earlier):
    return pl.pallas_call(
        both_kernel,
        out_shape=jax.ShapeDtypeStruct((peers, 2, *own.shape), own.dtype),
        in_specs=[VMEM, VMEM, ANY],
        out_specs=VMEM,
        cost_estimate=NO_COST,
        compiler_params=params(4),
        name="both",
    )(own, other, earlier)


def copied(moves, sem):
    handles = [pltpu.make_async_copy(*move, sem.at[i]) for i, move in enumerate(moves)]
    for handle in handles:
        handle.start()
    for handle in handles:
        handle.wait()


def step_call(kernel, shapes, moves, operands, name):
    return pl.pallas_call(
        kernel,
        out_shape=tuple(jax.ShapeDtypeStruct(shape, BF16) for shape in shapes),
        in_specs=[HBM] * len(operands),
        out_specs=(HBM,) * len(shapes),
        scratch_shapes=[pltpu.SemaphoreType.DMA((moves,))],
        cost_estimate=NO_COST,
        compiler_params=params(2),
        name=name,
    )(*operands)


def sides_kernel(ahead, back, earlier, left, right, sem):
    half = left.shape[2]
    copied([(ahead.at[:, :, :half], left), (back.at[:, :, half:], right)], sem)


def sides(ahead, back, earlier):
    count, rows, width = ahead.shape
    part = (count, rows, width // 2)
    return step_call(sides_kernel, [part, part], 2, [ahead, back, earlier], "sides")


def along_kernel(own, ahead, left, right, back, out, sem):
    half = left.shape[2]
    copied(
        [
            (own, out.at[0:1]),
            (ahead, out.at[1:2]),
            (left, out.at[2:3, :, :half]),
            (right, out.at[2:3, :, half:]),
            (back, out.at[3:4]),
        ],
        sem,
    )


def along(own, ahead, left, right, back):
    shape = (4, *own.shape[1:])
    return step_call(along_kernel, [shape], 5, [own, ahead, left, right, back], "along")[0]


def halves_kernel(place, grads, query, keep, send):
    core = place[0]
    train = grads[...].astype(F32).T
    rows = lax.broadcasted_iota(jnp.int32, query.shape, 0)
    wide = query[...].astype(F32)

    def half(which):
        parts = []
        for i in range(2):
            by = 2 * which + 2 * i
            rolled = wide if by == 0 else jnp.concatenate([wide[by:], wide[:by]], 0)
            mine = (rows >= 2 * which) & (rows < 2 * which + 2)
            start = 64 * which + 32 * i
            parts += [train[start : start + 32], jnp.where(mine, rolled, 0.0)]
        return jnp.concatenate(parts, 0)

    lower, upper = half(0), half(1)
    keep[...] = jnp.where(core == 0, lower, upper).astype(BF16)
    send[...] = jnp.where(core == 0, upper, lower).astype(BF16)


def token_halves(place, grads, query):
    shape = jax.ShapeDtypeStruct((80, grads.shape[1]), BF16)
    return pl.pallas_call(
        halves_kernel,
        out_shape=(shape, shape),
        in_specs=[SMEM, VMEM, VMEM],
        out_specs=(VMEM, VMEM),
        cost_estimate=NO_COST,
        compiler_params=params(4),
        name="token_halves",
    )(place, grads.T, query)


def rotate_out_kernel(place, tokens, basis_own, basis_other, earlier, out):
    x = place[1]
    width = tokens.shape[3]
    for part in range(4):
        rows = slice(2 * part, 2 * part + 2)
        product = jnp.dot(
            tokens[rows, 0].reshape(-1, width), basis_own[...], preferred_element_type=F32
        ) + jnp.dot(
            tokens[rows, 1].reshape(-1, width), basis_other[...], preferred_element_type=F32
        )
        product = (product * SCALE_OUT).reshape(4, 40, -1)
        for z in range(4):
            out[(part - x + 4) % 4, z] = product[z]


def rotated_out(place, tokens, basis_own, basis_other, earlier):
    width = basis_own.shape[1]
    return pl.pallas_call(
        rotate_out_kernel,
        out_shape=jax.ShapeDtypeStruct((4, 4, 40, width), F32),
        in_specs=[SMEM, VMEM, VMEM, VMEM, ANY],
        out_specs=VMEM,
        cost_estimate=NO_COST,
        compiler_params=params(6),
        name="rotated_out",
    )(place, tokens, basis_own, basis_other, earlier)


def rotate_in_kernel(count, place, earlier, *refs):
    pieces, (own, other) = refs[:count], refs[count : count + 2]
    out, tokens, queries, basis, sem = refs[count + 2 :]
    zh = place[2]
    width, depth = own.shape
    half = depth // 2
    moves, at = [], 0
    for piece in pieces:
        blocks = piece.shape[0]
        if piece.shape[2] == depth:
            moves.append((piece, tokens.at[at : at + blocks]))
            at += blocks
        elif len(moves) % 2 == 0:
            moves.append((piece, tokens.at[at : at + blocks, :, :half]))
        else:
            moves.append((piece, tokens.at[at : at + blocks, :, half:]))
            at += blocks
    moves.append((own, basis.at[:width]))
    moves.append((other, basis.at[width:]))
    handles = [pltpu.make_async_copy(*move, sem.at[i]) for i, move in enumerate(moves)]
    for handle in handles:
        handle.start()
    for handle in handles[:-1]:
        handle.wait()
    for group in range(at // 4):
        for pair in range(2):
            first, second = ((2 * pair + i - zh + 4) % 4 for i in range(2))
            queries[2 * group + pair] = (
                tokens[4 * group + first, 32:, :].astype(F32)
                + tokens[4 * group + second, 32:, :].astype(F32)
            )
    rows = jnp.concatenate(
        [tokens[:, :32, :].reshape(-1, depth), queries[...].reshape(-1, depth).astype(BF16)], 0
    )
    split = at * 32
    for start in range(0, 2 * width, 256):
        stop = min(start + 256, 2 * width)
        if start < width < stop:
            handles[-1].wait()
        product = lax.dot_general(rows, basis[start:stop, :], LAST_LAST, preferred_element_type=F32)
        product = product * SCALE_IN
        out[:, :64, start:stop] = product[:split].reshape(-1, 64, stop - start)
        out[:, 64:, start:stop] = product[split:].reshape(-1, 8, stop - start)


def rotated_in(place, pieces, own, other, earlier):
    count = len(pieces)
    width, depth = own.shape
    blocks = sum(piece.size for piece in pieces) // (40 * depth)
    return pl.pallas_call(
        functools.partial(rotate_in_kernel, count),
        out_shape=jax.ShapeDtypeStruct((blocks // 2, 72, 2 * width), F32),
        in_specs=[SMEM, ANY] + [HBM] * (count + 2),
        out_specs=VMEM,
        scratch_shapes=[
            pltpu.VMEM((blocks, 40, depth), BF16),
            pltpu.VMEM((blocks // 2, 8, depth), F32),
            pltpu.VMEM((2 * width, depth), BF16),
            pltpu.SemaphoreType.DMA((count + 2,)),
        ],
        cost_estimate=NO_COST,
        compiler_params=params(24),
        name="rotated_in",
    )(place, earlier, *pieces, own, other)


def final_kernel(place, damping, acts, *refs):
    grads_own, grads_other, out = refs[:4], refs[4:8], refs[8]
    core, x, zh = place[0], place[1], place[2]
    width, height = out.shape
    tile = 192

    for left in range(0, width, tile):
        cols = slice(left, min(left + tile, width))
        total = None
        query_act, query_grad = [], []
        for step in range(4):
            for pair in range(2):
                places = [(2 * pair + half - zh + 4) % 4 for half in range(2)]
                for source, part in ((grads_own[step], core), (grads_other[step], 1 - core)):
                    slot = (2 * pair + part - zh + 4) % 4
                    share = 2 * step + slot // 2
                    rows = pl.ds(pl.multiple_of(slot % 2 * 32, 32), 32)
                    act = jnp.concatenate([acts[share, half, rows, cols] for half in range(2)], 0)
                    grad = jnp.concatenate([source[at, :32, :] for at in places], 0)
                    outer = lax.dot_general(act, grad, TOKENS_FIRST, preferred_element_type=F32)
                    total = outer * outer if total is None else total + outer * outer
                for half, at in enumerate(places):
                    query_act.append(acts[2 * step + pair, half, 64:, cols])
                    query_grad.append(grads_own[step][at, 32:, :] + grads_other[step][at, 32:, :])
        query = lax.dot_general(
            jnp.concatenate(query_act, 0),
            jnp.concatenate(query_grad, 0),
            TOKENS_FIRST,
            preferred_element_type=F32,
        )
        out[cols, :] = query / (total * (1 / EXAMPLES) + damping[0])


def corrected(place, damping, acts, grads_own, grads_other):
    shape = (acts.shape[3], grads_own[0].shape[2])
    return pl.pallas_call(
        final_kernel,
        out_shape=jax.ShapeDtypeStruct(shape, F32),
        in_specs=[SMEM, SMEM] + [VMEM] * 9,
        out_specs=VMEM,
        cost_estimate=NO_COST,
        compiler_params=params(12),
        name="corrected",
    )(place, damping, acts, *grads_own, *grads_other)


def shards(activations, out_grads, query_acts, query_grads, basis_in, basis_out, damping):
    core, x, zh = (lax.axis_index(name) for name in ROW[2:] + ROW[:2])
    place = jnp.stack([core, x, zh]).astype(jnp.int32)
    width_in = basis_in.shape[1]

    group = jnp.where(
        zh % 2 == 0,
        jnp.pad(query_acts, ((0, 6), (0, 0))),
        jnp.pad(query_acts, ((2, 4), (0, 0))),
    )
    own = jnp.concatenate([activations, group], 0)[None]
    z_ahead = from_ahead(own, "zh", 1)
    z_back = from_ahead(own, "zh", -1)

    columns_own = basis_in.T
    columns_other = swapped(columns_own)
    basis_out_other = swapped(basis_out)

    keep, send = token_halves(place, out_grads, query_grads)
    received = swapped(send)

    left, right = sides(z_ahead, z_back, received)
    z_left = from_ahead(left, "zh", 1)
    z_right = from_ahead(right, "zh", -1)
    row = along(own, z_ahead, z_left, z_right, z_back)
    x_ahead = from_ahead(row, "x", 1)
    x_back = from_ahead(row, "x", -1)

    grads = exchanged(both_for_each(keep, received, 8, row), COL)
    partial_out = rotated_out(place, grads, basis_out, basis_out_other, row)

    left, right = sides(x_ahead, x_back, partial_out)
    x_left = from_ahead(left, "x", 1)
    x_right = from_ahead(right, "x", -1)

    early = rotated_in(place, [row, x_ahead, x_back], columns_own, columns_other, left)
    late = rotated_in(place, [x_left, x_right], columns_own, columns_other, early)
    partial_in = jnp.concatenate([early[:4], late, early[4:]], 0).astype(WIRE)
    arrived_in = exchanged(partial_in, COL)

    wire_out = partial_out[1:].astype(WIRE)
    sum_x = partial_out[0]
    for by in range(1, 4):
        sum_x = sum_x + from_ahead(wire_out[by - 1], "x", -by).astype(F32)
    sum_x = sum_x * (SCALE_OUT_X / SCALE_OUT)
    share_out = lax.dynamic_index_in_dim(sum_x, zh, 0, False)
    for by in range(1, 4):
        block = lax.dynamic_index_in_dim(sum_x, (zh + by) % 4, 0, False).astype(WIRE)
        share_out = share_out + from_ahead(block, "zh", -by).astype(F32)
    share_out = (share_out * (1 / SCALE_OUT_X)).astype(BF16)
    blocks = [share_out] + [from_ahead(share_out, "zh", by) for by in range(1, 4)]
    blocks = jnp.stack(blocks)
    grads_own = [blocks] + [from_ahead(blocks, "x", by) for by in range(1, 4)]
    grads_other = [swapped(value) for value in grads_own]

    share_in = (arrived_in.astype(F32).sum(0) * (1 / SCALE_IN)).astype(BF16)
    own = share_in[:, :width_in]
    other = swapped(share_in[:, width_in:])
    acts = exchanged(shares_for_each(place, own, other, 8, blocks), COL)

    return corrected(place, damping, acts, grads_own, grads_other).T


def solution(mesh):
    finer = Mesh(mesh.devices.reshape(4, 4, 2, 4, 2), (*ROW, *COL))
    placed = (
        P(ROW, COL),
        P(COL, ROW),
        P(ROW, COL),
        P(COL, ROW),
        P(COL, ROW),
        P(ROW, COL),
        P(),
    )
    return jax.shard_map(
        shards, mesh=finer, in_specs=placed, out_specs=P(COL, ROW), check_vma=False
    )
```

```python
import functools
import jax
import jax.numpy as jnp
from jax import lax
from jax.experimental import pallas as pl
from jax.experimental.pallas import tpu as pltpu
from jax.sharding import Mesh
from jax.sharding import PartitionSpec as P

EXAMPLES = 16
ROW = ("x", "zh", "core")
COL = ("y", "zl")
BF16 = jnp.bfloat16
WIRE = jnp.float16
F32 = jnp.float32
SCALE_IN = 2.0**6
SCALE_OUT = 2.0**11
SCALE_OUT_X = 2.0**9
TOKENS_FIRST = (((0,), (0,)), ((), ()))
LAST_LAST = (((1,), (1,)), ((), ()))
VMEM = pl.BlockSpec(memory_space=pltpu.VMEM)
SMEM = pl.BlockSpec(memory_space=pltpu.SMEM)
ANY = pl.BlockSpec(memory_space=pl.ANY)
HBM = pl.BlockSpec(memory_space=pltpu.HBM)


NO_COST = pl.CostEstimate(flops=0, bytes_accessed=0, transcendentals=0)


def params(mib):
    return pltpu.CompilerParams(vmem_limit_bytes=mib * 2**20)


def from_ahead(value, axis, by):
    size = lax.axis_size(axis)
    return lax.ppermute(value, axis, [((i + by) % size, i) for i in range(size)])


def swapped(value):
    return from_ahead(value, "core", 1)


def exchanged(blocks, axis):
    return lax.all_to_all(blocks, axis, 0, 0, tiled=True)


def shares_kernel(place, own, other, earlier, out):
    first = place[0] == 0
    lower = jnp.where(first, own[...], other[...])
    upper = jnp.where(first, other[...], own[...])
    for peer in range(out.shape[0]):
        out[peer, 0] = lower
        out[peer, 1] = upper


def shares_for_each(place, own, other, peers, earlier):
    return pl.pallas_call(
        shares_kernel,
        out_shape=jax.ShapeDtypeStruct((peers, 2, *own.shape), own.dtype),
        in_specs=[SMEM, VMEM, VMEM, ANY],
        out_specs=VMEM,
        cost_estimate=NO_COST,
        compiler_params=params(4),
        name="shares",
    )(place, own, other, earlier)


def both_kernel(own, other, earlier, out):
    for peer in range(out.shape[0]):
        out[peer, 0] = own[...]
        out[peer, 1] = other[...]


def both_for_each(own, other, peers, earlier):
    return pl.pallas_call(
        both_kernel,
        out_shape=jax.ShapeDtypeStruct((peers, 2, *own.shape), own.dtype),
        in_specs=[VMEM, VMEM, ANY],
        out_specs=VMEM,
        cost_estimate=NO_COST,
        compiler_params=params(4),
        name="both",
    )(own, other, earlier)


def copied(moves, sem):
    handles = [pltpu.make_async_copy(*move, sem.at[i]) for i, move in enumerate(moves)]
    for handle in handles:
        handle.start()
    for handle in handles:
        handle.wait()


def step_call(kernel, shapes, moves, operands, name):
    return pl.pallas_call(
        kernel,
        out_shape=tuple(jax.ShapeDtypeStruct(shape, BF16) for shape in shapes),
        in_specs=[HBM] * len(operands),
        out_specs=(HBM,) * len(shapes),
        scratch_shapes=[pltpu.SemaphoreType.DMA((moves,))],
        cost_estimate=NO_COST,
        compiler_params=params(2),
        name=name,
    )(*operands)


def sides_kernel(ahead, back, earlier, left, right, sem):
    half = left.shape[2]
    copied([(ahead.at[:, :, :half], left), (back.at[:, :, half:], right)], sem)


def sides(ahead, back, earlier):
    count, rows, width = ahead.shape
    part = (count, rows, width // 2)
    return step_call(sides_kernel, [part, part], 2, [ahead, back, earlier], "sides")


def along_kernel(own, ahead, left, right, back, out, sem):
    half = left.shape[2]
    copied(
        [
            (own, out.at[0:1]),
            (ahead, out.at[1:2]),
            (left, out.at[2:3, :, :half]),
            (right, out.at[2:3, :, half:]),
            (back, out.at[3:4]),
        ],
        sem,
    )


def along(own, ahead, left, right, back):
    shape = (4, *own.shape[1:])
    return step_call(along_kernel, [shape], 5, [own, ahead, left, right, back], "along")[0]


def halves_kernel(place, grads, query, keep, send):
    core = place[0]
    train = grads[...].astype(F32).T
    rows = lax.broadcasted_iota(jnp.int32, query.shape, 0)
    wide = query[...].astype(F32)

    def half(which):
        parts = []
        for i in range(2):
            by = 2 * which + 2 * i
            rolled = wide if by == 0 else jnp.concatenate([wide[by:], wide[:by]], 0)
            mine = (rows >= 2 * which) & (rows < 2 * which + 2)
            start = 64 * which + 32 * i
            parts += [train[start : start + 32], jnp.where(mine, rolled, 0.0)]
        return jnp.concatenate(parts, 0)

    lower, upper = half(0), half(1)
    keep[...] = jnp.where(core == 0, lower, upper).astype(BF16)
    send[...] = jnp.where(core == 0, upper, lower).astype(BF16)


def token_halves(place, grads, query):
    shape = jax.ShapeDtypeStruct((80, grads.shape[1]), BF16)
    return pl.pallas_call(
        halves_kernel,
        out_shape=(shape, shape),
        in_specs=[SMEM, VMEM, VMEM],
        out_specs=(VMEM, VMEM),
        cost_estimate=NO_COST,
        compiler_params=params(4),
        name="token_halves",
    )(place, grads.T, query)


def rotate_out_kernel(place, tokens, basis_own, basis_other, earlier, out):
    x = place[1]
    width = tokens.shape[3]
    for part in range(4):
        rows = slice(2 * part, 2 * part + 2)
        product = jnp.dot(
            tokens[rows, 0].reshape(-1, width), basis_own[...], preferred_element_type=F32
        ) + jnp.dot(
            tokens[rows, 1].reshape(-1, width), basis_other[...], preferred_element_type=F32
        )
        product = (product * SCALE_OUT).reshape(4, 40, -1)
        for z in range(4):
            out[(part - x + 4) % 4, z] = product[z]


def rotated_out(place, tokens, basis_own, basis_other, earlier):
    width = basis_own.shape[1]
    return pl.pallas_call(
        rotate_out_kernel,
        out_shape=jax.ShapeDtypeStruct((4, 4, 40, width), F32),
        in_specs=[SMEM, VMEM, VMEM, VMEM, ANY],
        out_specs=VMEM,
        cost_estimate=NO_COST,
        compiler_params=params(6),
        name="rotated_out",
    )(place, tokens, basis_own, basis_other, earlier)


def rotate_in_kernel(count, place, earlier, *refs):
    pieces, (own, other) = refs[:count], refs[count : count + 2]
    out, tokens, queries, basis, sem = refs[count + 2 :]
    zh = place[2]
    width, depth = own.shape
    half = depth // 2
    moves, at = [], 0
    for piece in pieces:
        blocks = piece.shape[0]
        if piece.shape[2] == depth:
            moves.append((piece, tokens.at[at : at + blocks]))
            at += blocks
        elif len(moves) % 2 == 0:
            moves.append((piece, tokens.at[at : at + blocks, :, :half]))
        else:
            moves.append((piece, tokens.at[at : at + blocks, :, half:]))
            at += blocks
    moves.append((own, basis.at[:width]))
    moves.append((other, basis.at[width:]))
    handles = [pltpu.make_async_copy(*move, sem.at[i]) for i, move in enumerate(moves)]
    for handle in handles:
        handle.start()
    for handle in handles[:-1]:
        handle.wait()
    for group in range(at // 4):
        for pair in range(2):
            first, second = ((2 * pair + i - zh + 4) % 4 for i in range(2))
            queries[2 * group + pair] = (
                tokens[4 * group + first, 32:, :].astype(F32)
                + tokens[4 * group + second, 32:, :].astype(F32)
            )
    rows = jnp.concatenate(
        [tokens[:, :32, :].reshape(-1, depth), queries[...].reshape(-1, depth).astype(BF16)], 0
    )
    split = at * 32
    for start in range(0, 2 * width, 256):
        stop = min(start + 256, 2 * width)
        if start < width < stop:
            handles[-1].wait()
        product = lax.dot_general(rows, basis[start:stop, :], LAST_LAST, preferred_element_type=F32)
        product = product * SCALE_IN
        out[:, :64, start:stop] = product[:split].reshape(-1, 64, stop - start)
        out[:, 64:, start:stop] = product[split:].reshape(-1, 8, stop - start)


def rotated_in(place, pieces, own, other, earlier):
    count = len(pieces)
    width, depth = own.shape
    blocks = sum(piece.size for piece in pieces) // (40 * depth)
    return pl.pallas_call(
        functools.partial(rotate_in_kernel, count),
        out_shape=jax.ShapeDtypeStruct((blocks // 2, 72, 2 * width), F32),
        in_specs=[SMEM, ANY] + [HBM] * (count + 2),
        out_specs=VMEM,
        scratch_shapes=[
            pltpu.VMEM((blocks, 40, depth), BF16),
            pltpu.VMEM((blocks // 2, 8, depth), F32),
            pltpu.VMEM((2 * width, depth), BF16),
            pltpu.SemaphoreType.DMA((count + 2,)),
        ],
        cost_estimate=NO_COST,
        compiler_params=params(24),
        name="rotated_in",
    )(place, earlier, *pieces, own, other)


def final_kernel(place, damping, acts, *refs):
    grads_own, grads_other, out = refs[:4], refs[4:8], refs[8]
    core, x, zh = place[0], place[1], place[2]
    width, height = out.shape
    tile = 256

    for left in range(0, width, tile):
        cols = slice(left, min(left + tile, width))
        total = None
        query_act, query_grad = [], []
        for step in range(4):
            for pair in range(2):
                places = [(2 * pair + half - zh + 4) % 4 for half in range(2)]
                for source, part in ((grads_own[step], core), (grads_other[step], 1 - core)):
                    slot = (2 * pair + part - zh + 4) % 4
                    share = 2 * step + slot // 2
                    rows = pl.ds(pl.multiple_of(slot % 2 * 32, 32), 32)
                    act = jnp.concatenate([acts[share, half, rows, cols] for half in range(2)], 0)
                    grad = jnp.concatenate([source[at, :32, :] for at in places], 0)
                    outer = lax.dot_general(act, grad, TOKENS_FIRST, preferred_element_type=F32)
                    total = outer * outer if total is None else total + outer * outer
                for half, at in enumerate(places):
                    query_act.append(acts[2 * step + pair, half, 64:, cols])
                    query_grad.append(grads_own[step][at, 32:, :] + grads_other[step][at, 32:, :])
        query = lax.dot_general(
            jnp.concatenate(query_act, 0),
            jnp.concatenate(query_grad, 0),
            TOKENS_FIRST,
            preferred_element_type=F32,
        )
        out[cols, :] = query / (total * (1 / EXAMPLES) + damping[0])


def corrected(place, damping, acts, grads_own, grads_other):
    shape = (acts.shape[3], grads_own[0].shape[2])
    return pl.pallas_call(
        final_kernel,
        out_shape=jax.ShapeDtypeStruct(shape, F32),
        in_specs=[SMEM, SMEM] + [VMEM] * 9,
        out_specs=VMEM,
        cost_estimate=NO_COST,
        compiler_params=params(12),
        name="corrected",
    )(place, damping, acts, *grads_own, *grads_other)


def shards(activations, out_grads, query_acts, query_grads, basis_in, basis_out, damping):
    core, x, zh = (lax.axis_index(name) for name in ROW[2:] + ROW[:2])
    place = jnp.stack([core, x, zh]).astype(jnp.int32)
    width_in = basis_in.shape[1]

    group = jnp.where(
        zh % 2 == 0,
        jnp.pad(query_acts, ((0, 6), (0, 0))),
        jnp.pad(query_acts, ((2, 4), (0, 0))),
    )
    own = jnp.concatenate([activations, group], 0)[None]
    z_ahead = from_ahead(own, "zh", 1)
    z_back = from_ahead(own, "zh", -1)

    columns_own = basis_in.T
    columns_other = swapped(columns_own)
    basis_out_other = swapped(basis_out)

    keep, send = token_halves(place, out_grads, query_grads)
    received = swapped(send)

    left, right = sides(z_ahead, z_back, received)
    z_left = from_ahead(left, "zh", 1)
    z_right = from_ahead(right, "zh", -1)
    row = along(own, z_ahead, z_left, z_right, z_back)
    x_ahead = from_ahead(row, "x", 1)
    x_back = from_ahead(row, "x", -1)

    grads = exchanged(both_for_each(keep, received, 8, row), COL)
    partial_out = rotated_out(place, grads, basis_out, basis_out_other, row)

    left, right = sides(x_ahead, x_back, partial_out)
    x_left = from_ahead(left, "x", 1)
    x_right = from_ahead(right, "x", -1)

    early = rotated_in(place, [row, x_ahead, x_back], columns_own, columns_other, left)
    late = rotated_in(place, [x_left, x_right], columns_own, columns_other, early)
    partial_in = jnp.concatenate([early[:4], late, early[4:]], 0).astype(WIRE)
    arrived_in = exchanged(partial_in, COL)

    wire_out = partial_out[1:].astype(WIRE)
    sum_x = partial_out[0]
    for by in range(1, 4):
        sum_x = sum_x + from_ahead(wire_out[by - 1], "x", -by).astype(F32)
    sum_x = sum_x * (SCALE_OUT_X / SCALE_OUT)
    share_out = lax.dynamic_index_in_dim(sum_x, zh, 0, False)
    for by in range(1, 4):
        block = lax.dynamic_index_in_dim(sum_x, (zh + by) % 4, 0, False).astype(WIRE)
        share_out = share_out + from_ahead(block, "zh", -by).astype(F32)
    share_out = (share_out * (1 / SCALE_OUT_X)).astype(BF16)
    blocks = [share_out] + [from_ahead(share_out, "zh", by) for by in range(1, 4)]
    blocks = jnp.stack(blocks)
    grads_own = [blocks] + [from_ahead(blocks, "x", by) for by in range(1, 4)]
    grads_other = [swapped(value) for value in grads_own]

    share_in = (arrived_in.astype(F32).sum(0) * (1 / SCALE_IN)).astype(BF16)
    own = share_in[:, :width_in]
    other = swapped(share_in[:, width_in:])
    acts = exchanged(shares_for_each(place, own, other, 8, blocks), COL)

    return corrected(place, damping, acts, grads_own, grads_other).T


def solution(mesh):
    finer = Mesh(mesh.devices.reshape(4, 4, 2, 4, 2), (*ROW, *COL))
    placed = (
        P(ROW, COL),
        P(COL, ROW),
        P(ROW, COL),
        P(COL, ROW),
        P(COL, ROW),
        P(ROW, COL),
        P(),
    )
    return jax.shard_map(
        shards, mesh=finer, in_specs=placed, out_specs=P(COL, ROW), check_vma=False
    )
```
